32 devices in a mesh: user: 4 (over y, x), item: 8 (over z, core).
Axes of the slice: x: 2, y: 2, z: 4, core: 2. Of those that a mesh axis runs over, the one named last changes fastest.
Arguments:
- user_cot: bfloat16 [6144, 64], P(('user', 'item')), may hold values from -6 to 6
- item_cot: bfloat16 [16384, 64], P(('item', 'user')), may hold values from -6 to 6
- tile_weight: int32 [64, 2048, 256], P('user', 'item'), may hold values from 0 to 3
- tile_rows: int32 [4, 128], P('user', 'item'), may hold values from 0 to 5, as said below
- tile_cols: int32 [4, 128], P('user', 'item'), may hold values from 0 to 7, as said below
- tile_count: int32 [4, 8], P('user', 'item'), may hold values from 4 to 16, as said below
- user_degree: int32 [6144], P('user'), may hold values from 35 to 139
- item_degree: int32 [16384], P('item'), may hold values from 48 to 191
Outputs:
- user_grad: bfloat16 [6144, 64], P(('user', 'item'))
- item_grad: bfloat16 [16384, 64], P(('item', 'user'))
The draws below stay inside these ranges and needn't reach their ends.
Inputs may be any that keep to these rules, and one draw needn't show every extreme that they name: `tile_rows`: entries past a device's count are padding. Among a device's live slots no (row, column) pair repeats. `tile_cols`: paired with tile_rows slot by slot. `tile_count`: some device holds 16 live slots.
All inputs are finite; a program needn't handle non-finite values.
Results may differ from the reference program's by a relative error of at most 0.0034.
Values may be sent and summed in bfloat16 or wider, within the bound.
A program may use at most 64 MiB of HBM per device.

```python
import jax
import jax.numpy as jnp
from jax import lax

WIDTH = 64
TILE = 256
UB = 6
IB = 8
MAXT = 16
DEGIT = 48
USERS = 6144
ITEMS = 16384
DEGLO = 35
N_USER = 4
N_ITEM = 8


def block_lists(key):
    devices = N_USER * N_ITEM
    key_list = jax.random.split(jax.random.fold_in(key, 11), devices)
    orders = jax.vmap(lambda key_one: jax.random.permutation(key_one, UB * IB))(key_list)[:, :MAXT]
    return orders.reshape(N_USER, N_ITEM * MAXT).astype(jnp.int32)


def draw_tile_rows(key, part):
    return (block_lists(key) // IB).astype(jnp.int32)


def draw_tile_cols(key, part):
    return (block_lists(key) % IB).astype(jnp.int32)


def draw_tile_count(key, part):
    devices = N_USER * N_ITEM
    extent = MAXT - MAXT // 4
    picks = jax.random.randint(jax.random.fold_in(key, 3), (devices,), 0, extent + 1)
    counts = MAXT // 4 + picks * picks // extent
    chosen = jax.random.randint(jax.random.fold_in(key, 5), (), 0, devices)
    counts = jnp.where(jnp.arange(devices, dtype=jnp.int32) == chosen, MAXT, counts)
    return counts.reshape(N_USER, N_ITEM).astype(jnp.int32)


def plant(array, own_key, smallest, high):
    shape = array.shape
    place = [jax.random.randint(jax.random.fold_in(own_key, axis), (), 0, shape[axis]) for axis in range(len(shape))]
    array = array.at[tuple(place)].set(smallest)
    longest = shape.index(max(shape))
    place[longest] = (place[longest] + 1) % shape[longest]
    return array.at[tuple(place)].set(high)


def shard_levels(rng, dims, shards, low, high):
    factor_of = 1.0
    for axis_at, blocks in shards:
        draws = jax.random.uniform(jax.random.fold_in(jax.random.fold_in(rng, 6), axis_at), (blocks,), jnp.float32, low / len(shards), high / len(shards))
        factor_of = factor_of * jnp.repeat(jnp.exp(draws), dims[axis_at] // blocks).reshape((-1,) + (1,) * (len(dims) - 1 - axis_at))
    return factor_of


def noise(stream_key, shape, width, limit, cuts=(), kind=jnp.bfloat16):
    factor_of = shard_levels(stream_key, shape, cuts, -0.22, 0.18) if cuts else 1.0
    drawn = jax.random.normal(stream_key, shape, jnp.float32) * width * factor_of
    return jnp.minimum(jnp.maximum(drawn, -limit), limit).astype(kind)


def setup_inputs(seed: int = 0) -> dict:
    splits = jax.random.split(jax.random.key(seed), 9)
    return {
        "user_cot": noise(splits[0], (USERS, WIDTH), 1.0, 6.0, ((0, 32),)),
        "item_cot": noise(splits[1], (ITEMS, WIDTH), 1.0, 6.0, ((0, 32),)),
        "tile_weight": plant(jax.random.randint(splits[2], (N_USER * MAXT, N_ITEM * TILE, TILE), 0, 4), jax.random.fold_in(splits[2], 1), 0, 3).astype(jnp.int32),
        "tile_rows": draw_tile_rows(jax.random.fold_in(splits[8], 71), 0),
        "tile_cols": draw_tile_cols(jax.random.fold_in(splits[8], 71), 0),
        "tile_count": draw_tile_count(jax.random.fold_in(splits[8], 71), 0),
        "user_degree": plant(jax.random.randint(splits[6], (USERS,), DEGLO, 4 * DEGLO), jax.random.fold_in(splits[6], 1), DEGLO, (4 * DEGLO) - 1).astype(jnp.int32),
        "item_degree": plant(jax.random.randint(splits[7], (ITEMS,), DEGIT, 4 * DEGIT), jax.random.fold_in(splits[7], 1), DEGIT, (4 * DEGIT) - 1).astype(jnp.int32),
    }


def build_tiles(weights, row_ids, col_ids, live_count, user_deg, item_deg):
    tile_slots, tile_size = (weights.shape[0], weights.shape[2])
    row_scale = lax.rsqrt(user_deg.astype(jnp.float32)).reshape(-1, tile_size)
    col_scale = lax.rsqrt(item_deg.astype(jnp.float32)).reshape(-1, tile_size)
    row_onehot = (row_ids[:, None] == jnp.arange(row_scale.shape[0], dtype=jnp.int32)[None, :]).astype(jnp.float32)
    col_onehot = (col_ids[:, None] == jnp.arange(col_scale.shape[0], dtype=jnp.int32)[None, :]).astype(jnp.float32)
    live_mask = (jnp.arange(tile_slots, dtype=jnp.int32) < live_count).astype(jnp.float32)
    row_factor = jnp.dot(row_onehot, row_scale, precision=lax.Precision.HIGHEST) * live_mask[:, None]
    col_factor = jnp.dot(col_onehot, col_scale, precision=lax.Precision.HIGHEST)
    adjacency = (weights.astype(jnp.float32) * row_factor[:, :, None] * col_factor[:, None, :]).astype(jnp.bfloat16)
    return (adjacency, row_onehot, col_onehot)

def toward_items(adjacency, col_onehot, row_ids, user_rows):
    tile_size = adjacency.shape[1]
    panel = user_rows.reshape(-1, tile_size, user_rows.shape[1])
    blocks = jnp.take(panel, row_ids, axis=0)
    contrib = jnp.einsum('trc,trd->tcd', adjacency.astype(jnp.float32), blocks.astype(jnp.float32), precision=lax.Precision.HIGHEST)
    summed = jnp.einsum('tb,tcd->bcd', col_onehot, contrib, precision=lax.Precision.HIGHEST)
    return summed.reshape(-1, user_rows.shape[1])

def toward_users(adjacency, row_onehot, col_ids, item_rows):
    tile_size = adjacency.shape[1]
    panel = item_rows.reshape(-1, tile_size, item_rows.shape[1])
    blocks = jnp.take(panel, col_ids, axis=0)
    contrib = jnp.einsum('trc,tcd->trd', adjacency.astype(jnp.float32), blocks.astype(jnp.float32), precision=lax.Precision.HIGHEST)
    summed = jnp.einsum('tb,trd->brd', row_onehot, contrib, precision=lax.Precision.HIGHEST)
    return summed.reshape(-1, item_rows.shape[1])

def reference(user_cot, item_cot, tile_weight, tile_rows, tile_cols, tile_count, user_degree, item_degree):
    emb_width = user_cot.shape[1]
    shard_users = UB * TILE
    shard_items = IB * TILE

    def propagate(user_panel, item_panel):

        def visit(running, device):
            to_item, to_user = running
            user_shard = device // N_ITEM
            item_shard = device % N_ITEM
            weights = lax.dynamic_slice(tile_weight, (user_shard * MAXT, item_shard * TILE, user_shard * 0), (MAXT, TILE, TILE))
            row_ids = lax.dynamic_slice(tile_rows, (user_shard, item_shard * MAXT), (1, MAXT))[0]
            col_ids = lax.dynamic_slice(tile_cols, (user_shard, item_shard * MAXT), (1, MAXT))[0]
            live_count = lax.dynamic_slice(tile_count, (user_shard, item_shard), (1, 1))[0, 0]
            user_deg = lax.dynamic_slice_in_dim(user_degree, user_shard * shard_users, shard_users, 0)
            item_deg = lax.dynamic_slice_in_dim(item_degree, item_shard * shard_items, shard_items, 0)
            adjacency, row_onehot, col_onehot = build_tiles(weights, row_ids, col_ids, live_count, user_deg, item_deg)
            user_rows = lax.dynamic_slice_in_dim(user_panel, user_shard * shard_users, shard_users, 0)
            item_rows = lax.dynamic_slice_in_dim(item_panel, item_shard * shard_items, shard_items, 0)
            item_part = toward_items(adjacency, col_onehot, row_ids, user_rows)
            user_part = toward_users(adjacency, row_onehot, col_ids, item_rows)
            old_item = lax.dynamic_slice_in_dim(to_item, item_shard * shard_items, shard_items, 0)
            to_item = lax.dynamic_update_slice_in_dim(to_item, old_item + item_part, item_shard * shard_items, 0)
            old_user = lax.dynamic_slice_in_dim(to_user, user_shard * shard_users, shard_users, 0)
            to_user = lax.dynamic_update_slice_in_dim(to_user, old_user + user_part, user_shard * shard_users, 0)
            return ((to_item, to_user), None)
        zero_pair = (jnp.zeros((item_panel.shape[0], emb_width), jnp.float32), jnp.zeros((user_panel.shape[0], emb_width), jnp.float32))
        (to_item, to_user), unused = lax.scan(visit, zero_pair, jnp.arange(N_USER * N_ITEM, dtype=jnp.int32))
        return (to_item, to_user)
    once_item, once_user = propagate(user_cot, item_cot)
    once_item = once_item.astype(jnp.bfloat16)
    once_user = once_user.astype(jnp.bfloat16)
    twice_item, twice_user = propagate(once_user, once_item)
    user_grad = ((user_cot.astype(jnp.float32) + once_user.astype(jnp.float32) + twice_user) / 3.0).astype(jnp.bfloat16)
    item_grad = ((item_cot.astype(jnp.float32) + once_item.astype(jnp.float32) + twice_item) / 3.0).astype(jnp.bfloat16)
    return (user_grad, item_grad)
```

```python
import functools

import jax
import jax.numpy as jnp
from jax import lax
from jax.experimental import pallas as pl
from jax.experimental.pallas import tpu as pltpu
from jax.sharding import PartitionSpec as P

F32 = jnp.float32
BF16 = jnp.bfloat16
MESH = pl.DeviceIdType.MESH


def kernel(
    sizes, user_cot, item_cot, weight, rows, cols, count, user_deg, item_deg,
    user_grad, item_grad,
    raw, adj, adj_t, row_scale, col_scale, user_panel, item_panel, to_user, to_item,
    user_flat, user_pack, item_pack,
    ag_user, ag_item, out_user, out_item, in_user, in_item,
    load_sem, ag_send_u, ag_recv_u, ag_send_i, ag_recv_i, rs_send_u, rs_recv_u, rs_send_i, rs_recv_i,
):
    n_user, n_item, slots, tile, width, row_tiles, col_tiles = sizes
    me_u, me_i = lax.axis_index("user"), lax.axis_index("item")
    half_u, half_i = user_pack.shape[1], item_pack.shape[1]

    for t in range(slots):
        pltpu.make_async_copy(weight.at[t], raw.at[t], load_sem.at[t]).start()

    barrier = pltpu.get_barrier_semaphore()

    def greet(axis, me, n):
        def step(k, carry):
            pl.semaphore_signal(
                barrier, inc=1, device_id={axis: lax.rem(me + k, n)}, device_id_type=MESH
            )
            return carry
        lax.fori_loop(1, n, step, 0)

    greet("item", me_i, n_item)
    greet("user", me_u, n_user)

    def pack(lo, hi):
        return jnp.concatenate([lo, hi], axis=1)

    own_u = pack(user_cot[0:half_u, :], user_cot[half_u : 2 * half_u, :])
    own_i = pack(item_cot[0:half_i, :], item_cot[half_i : 2 * half_i, :])
    user_pack[0] = own_u
    item_pack[0] = own_i
    ag_user[0, me_i] = own_u
    ag_item[0, me_u] = own_i

    pl.semaphore_wait(barrier, n_user + n_item - 2)

    def gather_copy(axis, me, n, buf, send, recv, hop, k):
        there = lax.rem(me + k, n)
        return pltpu.make_async_remote_copy(
            src_ref=buf.at[hop, me], dst_ref=buf.at[hop, me],
            send_sem=send.at[hop, there], recv_sem=recv.at[hop, me],
            device_id={axis: there}, device_id_type=MESH,
        )

    def gather_wait(axis, me, n, buf, send, recv, hop, k):
        there = lax.rem(me + k, n)
        return pltpu.make_async_remote_copy(
            src_ref=buf.at[hop, me], dst_ref=buf.at[hop, there],
            send_sem=send.at[hop, there], recv_sem=recv.at[hop, there],
            device_id={axis: there}, device_id_type=MESH,
        )

    def settle_copy(axis, me, n, src, dst, send, recv, hop, k):
        there = lax.rem(me + k, n)
        return pltpu.make_async_remote_copy(
            src_ref=src.at[hop, there], dst_ref=dst.at[hop, me],
            send_sem=send.at[hop, there], recv_sem=recv.at[hop, me],
            device_id={axis: there}, device_id_type=MESH,
        )

    def settle_wait(axis, me, n, src, dst, send, recv, hop, k):
        there = lax.rem(me + k, n)
        return pltpu.make_async_remote_copy(
            src_ref=src.at[hop, there], dst_ref=dst.at[hop, there],
            send_sem=send.at[hop, there], recv_sem=recv.at[hop, there],
            device_id={axis: there}, device_id_type=MESH,
        )

    AG_U = ("item", me_i, n_item, ag_user, ag_send_u, ag_recv_u)
    AG_I = ("user", me_u, n_user, ag_item, ag_send_i, ag_recv_i)
    RS_U = ("item", me_i, n_item, out_user, in_user, rs_send_u, rs_recv_u)
    RS_I = ("user", me_u, n_user, out_item, in_item, rs_send_i, rs_recv_i)

    def each(n, fn):
        def step(k, carry):
            fn(k)
            return carry
        lax.fori_loop(1, n, step, 0)

    def start_gather(g, hop):
        each(g[2], lambda k: gather_copy(*g, hop, k).start())

    def end_gather(g, hop):
        each(g[2], lambda k: gather_wait(*g, hop, k).wait_recv())

    def start_settle(s, hop):
        each(s[2], lambda k: settle_copy(*s, hop, k).start())

    def end_settle(s, hop):
        each(s[2], lambda k: settle_wait(*s, hop, k).wait_recv())

    start_gather(AG_U, 0)
    start_gather(AG_I, 0)

    for r in range(row_tiles):
        scale = lax.rsqrt(user_deg[:, r * tile : (r + 1) * tile].astype(F32))
        row_scale[r] = jnp.transpose(jnp.broadcast_to(scale, (128, tile)))
    for c in range(col_tiles):
        col_scale[c] = lax.rsqrt(item_deg[:, c * tile : (c + 1) * tile].astype(F32))
    row_id = [rows[0, t] for t in range(slots)]
    col_id = [cols[0, t] for t in range(slots)]

    def chain(ids, blocks):
        before = []
        for t in range(slots):
            prev = jnp.int32(slots)
            for s in range(t):
                prev = jnp.where(ids[s] == ids[t], jnp.int32(s), prev)
            before.append(prev)
        last = []
        for b in range(blocks):
            found = jnp.int32(slots)
            for t in range(slots):
                found = jnp.where(ids[t] == b, jnp.int32(t), found)
            last.append(found)
        return before, last

    row_before, row_last = chain(row_id, row_tiles)
    col_before, col_last = chain(col_id, col_tiles)
    to_user[slots] = jnp.zeros((tile, width), F32)
    to_item[slots] = jnp.zeros((tile, width), F32)
    live = count[0, 0]
    for t in range(slots):
        pltpu.make_async_copy(weight.at[t], raw.at[t], load_sem.at[t]).wait()
        on = jnp.where(t < live, jnp.float32(1), jnp.float32(0))
        rs = row_scale[row_id[t]]
        cs = col_scale[col_id[t]] * on
        w = raw[t].astype(F32)
        a = jnp.concatenate(
            [(w[:, j : j + 128] * rs) * cs[:, j : j + 128] for j in range(0, tile, 128)], axis=1
        ).astype(BF16)
        adj[t] = a
        adj_t[t] = jnp.transpose(a)

    def unpack(buf, hop, n, half, panel):
        for p in range(n):
            block = buf[hop, p]
            for side in range(2):
                part = block[:, side * width : (side + 1) * width]
                at, done = (2 * p + side) * half, 0
                while done < half:
                    b, off = divmod(at + done, tile)
                    size = min(half - done, tile - off)
                    panel[b, off : off + size, :] = part[done : done + size, :]
                    done += size

    def user_terms(hop):
        end_gather(AG_I, hop)
        unpack(ag_item, hop, n_user, half_i, item_panel)
        for t in range(slots):
            to_user[t] = to_user[row_before[t]] + jnp.dot(
                adj[t], item_panel[col_id[t]], preferred_element_type=F32
            )
        for r in range(row_tiles):
            user_flat[r * tile : (r + 1) * tile, :] = to_user[row_last[r]]
        for p in range(n_item):
            at = 2 * p * half_u
            out_user[hop, p] = pack(
                user_flat[at : at + half_u, :], user_flat[at + half_u : at + 2 * half_u, :]
            ).astype(out_user.dtype)
        in_user[hop, me_i] = out_user[hop, me_i]
        start_settle(RS_U, hop)

    def item_terms(hop):
        end_gather(AG_U, hop)
        unpack(ag_user, hop, n_item, half_u, user_panel)
        for t in range(slots):
            to_item[t] = to_item[col_before[t]] + jnp.dot(
                adj_t[t], user_panel[row_id[t]], preferred_element_type=F32
            )
        whole = [to_item[col_last[c]] for c in range(col_tiles)]

        def piece(at):
            b, off = divmod(at, tile)
            return whole[b][off : off + half_i, :]

        for p in range(n_user):
            out_item[hop, p] = pack(
                piece(2 * p * half_i), piece((2 * p + 1) * half_i)
            ).astype(out_item.dtype)
        in_item[hop, me_u] = out_item[hop, me_u]
        start_settle(RS_I, hop)

    def total(s, hop):
        end_settle(s, hop)
        dst = s[4]
        acc = dst[hop, 0].astype(F32)
        for p in range(1, s[2]):
            acc = acc + dst[hop, p].astype(F32)
        return acc

    user_terms(0)
    item_terms(0)
    once_i = total(RS_I, 0).astype(BF16)
    ag_item[1, me_u] = once_i
    start_gather(AG_I, 1)
    item_pack[1] = once_i
    once_u = total(RS_U, 0).astype(BF16)
    ag_user[1, me_i] = once_u
    start_gather(AG_U, 1)
    user_pack[1] = once_u
    user_terms(1)
    item_terms(1)

    def finish(s, packed, out, half):
        twice = total(s, 1)
        grad = ((packed[0].astype(F32) + packed[1].astype(F32) + twice) / 3.0).astype(BF16)
        out[0:half, :] = grad[:, 0:width]
        out[half : 2 * half, :] = grad[:, width : 2 * width]

    finish(RS_I, item_pack, item_grad, half_i)
    finish(RS_U, user_pack, user_grad, half_u)

    for hop in range(2):
        each(n_item, lambda k: gather_copy(*AG_U, hop, k).wait_send())
        each(n_user, lambda k: gather_copy(*AG_I, hop, k).wait_send())
        each(n_item, lambda k: settle_copy(*RS_U, hop, k).wait_send())
        each(n_user, lambda k: settle_copy(*RS_I, hop, k).wait_send())


def shards(n_user, n_item, user_cot, item_cot, tile_weight, tile_rows, tile_cols, tile_count, user_degree, item_degree):
    slots, tile = tile_weight.shape[0], tile_weight.shape[2]
    width = user_cot.shape[1]
    shard_users, shard_items = user_degree.shape[0], item_degree.shape[0]
    row_tiles, col_tiles = shard_users // tile, shard_items // tile
    half_u, half_i = user_cot.shape[0] // 2, item_cot.shape[0] // 2
    sizes = (n_user, n_item, slots, tile, width, row_tiles, col_tiles)
    sent = BF16
    vmem = pl.BlockSpec(memory_space=pltpu.VMEM)
    smem = pl.BlockSpec(memory_space=pltpu.SMEM)
    dma = pltpu.SemaphoreType.DMA
    return pl.pallas_call(
        functools.partial(kernel, sizes),
        out_shape=(
            jax.ShapeDtypeStruct(user_cot.shape, BF16),
            jax.ShapeDtypeStruct(item_cot.shape, BF16),
        ),
        in_specs=[vmem, vmem, pl.BlockSpec(memory_space=pl.ANY), smem, smem, smem, vmem, vmem],
        out_specs=(vmem, vmem),
        scratch_shapes=[
            pltpu.VMEM((slots, tile, tile), jnp.int32),
            pltpu.VMEM((slots, tile, tile), BF16),
            pltpu.VMEM((slots, tile, tile), BF16),
            pltpu.VMEM((row_tiles, tile, 128), F32),
            pltpu.VMEM((col_tiles, 1, tile), F32),
            pltpu.VMEM((row_tiles, tile, width), BF16),
            pltpu.VMEM((col_tiles, tile, width), BF16),
            pltpu.VMEM((slots + 1, tile, width), F32),
            pltpu.VMEM((slots + 1, tile, width), F32),
            pltpu.VMEM((shard_users, width), F32),
            pltpu.VMEM((2, half_u, 2 * width), BF16),
            pltpu.VMEM((2, half_i, 2 * width), BF16),
            pltpu.VMEM((2, n_item, half_u, 2 * width), BF16),
            pltpu.VMEM((2, n_user, half_i, 2 * width), BF16),
            pltpu.VMEM((2, n_item, half_u, 2 * width), sent),
            pltpu.VMEM((2, n_user, half_i, 2 * width), sent),
            pltpu.VMEM((2, n_item, half_u, 2 * width), sent),
            pltpu.VMEM((2, n_user, half_i, 2 * width), sent),
            dma((slots,)),
            dma((2, n_item)), dma((2, n_item)), dma((2, n_user)), dma((2, n_user)),
            dma((2, n_item)), dma((2, n_item)), dma((2, n_user)), dma((2, n_user)),
        ],
        compiler_params=pltpu.CompilerParams(
            collective_id=0, has_side_effects=True, vmem_limit_bytes=40 * 1024 * 1024
        ),
    )(
        user_cot, item_cot, tile_weight, tile_rows, tile_cols, tile_count,
        user_degree.reshape(1, shard_users), item_degree.reshape(1, shard_items),
    )


def solution(mesh):
    return jax.shard_map(
        functools.partial(shards, mesh.shape["user"], mesh.shape["item"]),
        mesh=mesh,
        in_specs=(
            P(("user", "item"), None),
            P(("item", "user"), None),
            P("user", "item", None),
            P("user", "item"),
            P("user", "item"),
            P("user", "item"),
            P("user"),
            P("item"),
        ),
        out_specs=(P(("user", "item"), None), P(("item", "user"), None)),
        check_vma=False,
    )
```

```python
import functools
import math

import jax
import jax.numpy as jnp
from jax import lax
from jax.experimental import pallas as pl
from jax.experimental.pallas import tpu as pltpu
from jax.sharding import PartitionSpec as P

F32 = jnp.float32
BF16 = jnp.bfloat16
MESH = pl.DeviceIdType.MESH


def kernel(
    sizes, user_cot, item_cot, weight, rows_in, cols_in, count_in, user_deg, item_deg,
    user_grad, item_grad,
    cot_u, cot_i, deg_u, deg_i, rows, cols, count,
    raw, adj, row_scale, col_scale, user_panel, item_panel, to_user, to_item,
    user_pack, item_pack,
    ag_user, ag_item, out_user, out_item, in_user, in_item,
    load_sem, small_sem, ag_send_u, ag_recv_u, ag_send_i, ag_recv_i, rs_send_u, rs_recv_u, rs_send_i, rs_recv_i,
):
    n_user, n_item, slots, tile, width, row_tiles, col_tiles = sizes
    me_u, me_i = lax.axis_index("user"), lax.axis_index("item")
    piece_u, piece_i = cot_u.shape[1], cot_i.shape[1]

    small = [
        pltpu.make_async_copy(src, dst, small_sem.at[j])
        for j, (src, dst) in enumerate([
            (user_cot, cot_u), (item_cot, cot_i), (user_deg, deg_u), (item_deg, deg_i),
            (rows_in, rows), (cols_in, cols), (count_in, count),
        ])
    ]
    for copy in small:
        copy.start()
    for t in range(slots):
        pltpu.make_async_copy(weight.at[t], raw.at[t], load_sem.at[t]).start()

    barrier = pltpu.get_barrier_semaphore()

    def greet(axis, me, n):
        def step(k, carry):
            pl.semaphore_signal(
                barrier, inc=1, device_id={axis: lax.rem(me + k, n)}, device_id_type=MESH
            )
            return carry
        lax.fori_loop(1, n, step, 0)

    greet("item", me_i, n_item)
    greet("user", me_u, n_user)

    grain = math.gcd(piece_u, 128)
    folds, whole_lanes = 128 // grain, piece_u // 128 * 128
    fold_rows, main_rows = width // folds, width * (piece_u // 128)

    def fold_in(put, take):
        for j in range(0, whole_lanes, 128):
            put(j // 128 * width, take(j, 128))
        if whole_lanes < piece_u:
            rest = take(whole_lanes, grain)
            put(main_rows, jnp.concatenate(
                [rest[f * fold_rows : (f + 1) * fold_rows, :] for f in range(folds)], axis=1))

    def unfold(wire, lane, size):
        if lane < whole_lanes:
            at = lane // 128 * width
            return wire[at : at + width, lane % 128 : lane % 128 + size]
        rest = wire[main_rows : main_rows + fold_rows, :]
        return jnp.concatenate(
            [rest[:, f * grain : (f + 1) * grain] for f in range(folds)], axis=0)

    for copy in small[:2]:
        copy.wait()
    own = cot_u[...]

    def put_own(at, value):
        user_pack[0, at : at + value.shape[0], :] = value

    fold_in(put_own, lambda lane, size: own[:, lane : lane + size])
    item_pack[0] = cot_i[...]
    ag_user[0, me_i] = user_pack[0]
    ag_item[0, me_u] = item_pack[0]

    pl.semaphore_wait(barrier, n_user + n_item - 2)

    def gather_copy(axis, me, n, buf, send, recv, hop, k):
        there = lax.rem(me + k, n)
        return pltpu.make_async_remote_copy(
            src_ref=buf.at[hop, me], dst_ref=buf.at[hop, me],
            send_sem=send.at[hop, there], recv_sem=recv.at[hop, me],
            device_id={axis: there}, device_id_type=MESH,
        )

    def gather_wait(axis, me, n, buf, send, recv, hop, k):
        there = lax.rem(me + k, n)
        return pltpu.make_async_remote_copy(
            src_ref=buf.at[hop, me], dst_ref=buf.at[hop, there],
            send_sem=send.at[hop, there], recv_sem=recv.at[hop, there],
            device_id={axis: there}, device_id_type=MESH,
        )

    def settle_copy(axis, me, n, src, dst, send, recv, hop, k):
        there = lax.rem(me + k, n)
        return pltpu.make_async_remote_copy(
            src_ref=src.at[hop, there], dst_ref=dst.at[hop, me],
            send_sem=send.at[hop, there], recv_sem=recv.at[hop, me],
            device_id={axis: there}, device_id_type=MESH,
        )

    def settle_wait(axis, me, n, src, dst, send, recv, hop, k):
        there = lax.rem(me + k, n)
        return pltpu.make_async_remote_copy(
            src_ref=src.at[hop, there], dst_ref=dst.at[hop, there],
            send_sem=send.at[hop, there], recv_sem=recv.at[hop, there],
            device_id={axis: there}, device_id_type=MESH,
        )

    AG_U = ("item", me_i, n_item, ag_user, ag_send_u, ag_recv_u)
    AG_I = ("user", me_u, n_user, ag_item, ag_send_i, ag_recv_i)
    RS_U = ("item", me_i, n_item, out_user, in_user, rs_send_u, rs_recv_u)
    RS_I = ("user", me_u, n_user, out_item, in_item, rs_send_i, rs_recv_i)

    def each(n, fn):
        def step(k, carry):
            fn(k)
            return carry
        lax.fori_loop(1, n, step, 0)

    def start_gather(g, hop):
        each(g[2], lambda k: gather_copy(*g, hop, k).start())

    def end_gather(g, hop):
        each(g[2], lambda k: gather_wait(*g, hop, k).wait_recv())

    def start_settle(s, hop):
        each(s[2], lambda k: settle_copy(*s, hop, k).start())

    def end_settle(s, hop):
        each(s[2], lambda k: settle_wait(*s, hop, k).wait_recv())

    start_gather(AG_U, 0)
    start_gather(AG_I, 0)

    for copy in small[2:]:
        copy.wait()
    for r in range(row_tiles):
        scale = lax.rsqrt(deg_u[r * tile : (r + 1) * tile].astype(F32)).reshape(1, tile)
        row_scale[r] = jnp.transpose(jnp.broadcast_to(scale, (128, tile)))
    for c in range(col_tiles):
        col_scale[c] = lax.rsqrt(deg_i[c * tile : (c + 1) * tile].astype(F32)).reshape(1, tile)
    row_id = [rows[0, t] for t in range(slots)]
    col_id = [cols[0, t] for t in range(slots)]

    def chain(ids, blocks):
        before = []
        for t in range(slots):
            prev = jnp.int32(slots)
            for s in range(t):
                prev = jnp.where(ids[s] == ids[t], jnp.int32(s), prev)
            before.append(prev)
        last = []
        for b in range(blocks):
            found = jnp.int32(slots)
            for t in range(slots):
                found = jnp.where(ids[t] == b, jnp.int32(t), found)
            last.append(found)
        return before, last

    row_before, row_last = chain(row_id, row_tiles)
    col_before, col_last = chain(col_id, col_tiles)
    to_user[slots] = jnp.zeros((width, tile), F32)
    to_item[slots] = jnp.zeros((width, tile), F32)
    live = count[0, 0]
    for t in range(slots):
        pltpu.make_async_copy(weight.at[t], raw.at[t], load_sem.at[t]).wait()
        on = jnp.where(t < live, jnp.float32(1), jnp.float32(0))
        rs = row_scale[row_id[t]]
        cs = col_scale[col_id[t]] * on
        w = raw[t].astype(F32)
        a = jnp.concatenate(
            [(w[:, j : j + 128] * rs) * cs[:, j : j + 128] for j in range(0, tile, 128)], axis=1
        ).astype(BF16)
        adj[t] = a

    def user_terms(hop):
        end_gather(AG_I, hop)
        for p in range(n_user):
            for lane in range(0, piece_i, 128):
                b, off = divmod(p * piece_i + lane, tile)
                item_panel[b, :, off : off + 128] = ag_item[hop, p, :, lane : lane + 128]
        for t in range(slots):
            to_user[t] = to_user[row_before[t]] + lax.dot_general(
                item_panel[col_id[t]], adj[t], (((1,), (1,)), ((), ())),
                preferred_element_type=F32,
            )
        tiles = [to_user[row_last[r]].astype(out_user.dtype) for r in range(row_tiles)]

        def lanes(at, size):
            parts = []
            while size:
                b, off = divmod(at, tile)
                step = size if off % 128 == 0 and off + size <= tile else grain
                parts.append(tiles[b][:, off : off + step])
                at, size = at + step, size - step
            return parts[0] if len(parts) == 1 else jnp.concatenate(parts, axis=1)

        for p in range(n_item):
            def put(at, value):
                out_user[hop, p, at : at + value.shape[0], :] = value

            fold_in(put, lambda lane, size: lanes(p * piece_u + lane, size))
        in_user[hop, me_i] = out_user[hop, me_i]
        start_settle(RS_U, hop)

    def item_terms(hop):
        end_gather(AG_U, hop)
        wires = [ag_user[hop, p] for p in range(n_item)]
        for at in range(0, n_item * piece_u, 128):
            p, lane = divmod(at, piece_u)
            if lane % 128 == 0 and lane < whole_lanes:
                block = unfold(wires[p], lane, 128)
            else:
                parts = []
                for g in range(at, at + 128, grain):
                    p, lane = divmod(g, piece_u)
                    parts.append(unfold(wires[p], lane, grain))
                block = jnp.concatenate(parts, axis=1)
            b, off = divmod(at, tile)
            user_panel[b, :, off : off + 128] = block
        for t in range(slots):
            to_item[t] = to_item[col_before[t]] + jnp.dot(
                user_panel[row_id[t]], adj[t], preferred_element_type=F32
            )
        for c in range(col_tiles):
            done = to_item[col_last[c]].astype(out_item.dtype)
            for lane in range(0, tile, 128):
                p, off = divmod(c * tile + lane, piece_i)
                out_item[hop, p, :, off : off + 128] = done[:, lane : lane + 128]
        in_item[hop, me_u] = out_item[hop, me_u]
        start_settle(RS_I, hop)

    def total(s, hop):
        end_settle(s, hop)
        dst = s[4]
        acc = dst[hop, 0].astype(F32)
        for p in range(1, s[2]):
            acc = acc + dst[hop, p].astype(F32)
        return acc

    user_terms(0)
    item_terms(0)
    once_i = total(RS_I, 0).astype(BF16)
    ag_item[1, me_u] = once_i
    start_gather(AG_I, 1)
    item_pack[1] = once_i
    once_u = total(RS_U, 0).astype(BF16)
    ag_user[1, me_i] = once_u
    start_gather(AG_U, 1)
    user_pack[1] = once_u
    user_terms(1)
    item_terms(1)

    def finish(s, packed):
        twice = total(s, 1)
        return ((packed[0].astype(F32) + packed[1].astype(F32) + twice) / 3.0).astype(BF16)

    item_grad[...] = finish(RS_I, item_pack)
    wire = finish(RS_U, user_pack)
    for lane in range(0, whole_lanes, 128):
        user_grad[:, lane : lane + 128] = unfold(wire, lane, 128)
    if whole_lanes < piece_u:
        user_grad[:, whole_lanes:piece_u] = unfold(wire, whole_lanes, grain)

    for hop in range(2):
        each(n_item, lambda k: gather_copy(*AG_U, hop, k).wait_send())
        each(n_user, lambda k: gather_copy(*AG_I, hop, k).wait_send())
        each(n_item, lambda k: settle_copy(*RS_U, hop, k).wait_send())
        each(n_user, lambda k: settle_copy(*RS_I, hop, k).wait_send())


def shards(n_user, n_item, user_cot, item_cot, tile_weight, tile_rows, tile_cols, tile_count, user_degree, item_degree):
    slots, tile = tile_weight.shape[0], tile_weight.shape[2]
    width = user_cot.shape[1]
    shard_users, shard_items = user_degree.shape[0], item_degree.shape[0]
    row_tiles, col_tiles = shard_users // tile, shard_items // tile
    piece_u, piece_i = user_cot.shape[0], item_cot.shape[0]
    wire_u = (width * piece_u // 128, 128)
    wire_i = (width, piece_i)
    sizes = (n_user, n_item, slots, tile, width, row_tiles, col_tiles)
    sent = BF16
    vmem = pl.BlockSpec(memory_space=pltpu.VMEM)
    dma = pltpu.SemaphoreType.DMA
    user_grad, item_grad = pl.pallas_call(
        functools.partial(kernel, sizes),
        out_shape=(
            jax.ShapeDtypeStruct((width, piece_u), BF16),
            jax.ShapeDtypeStruct((width, piece_i), BF16),
        ),
        in_specs=[pl.BlockSpec(memory_space=pl.ANY)] * 8,
        out_specs=(vmem, vmem),
        scratch_shapes=[
            pltpu.VMEM((width, piece_u), BF16),
            pltpu.VMEM((width, piece_i), BF16),
            pltpu.VMEM((shard_users,), jnp.int32),
            pltpu.VMEM((shard_items,), jnp.int32),
            pltpu.SMEM(tile_rows.shape, jnp.int32),
            pltpu.SMEM(tile_cols.shape, jnp.int32),
            pltpu.SMEM(tile_count.shape, jnp.int32),
            pltpu.VMEM((slots, tile, tile), jnp.int32),
            pltpu.VMEM((slots, tile, tile), BF16),
            pltpu.VMEM((row_tiles, tile, 128), F32),
            pltpu.VMEM((col_tiles, 1, tile), F32),
            pltpu.VMEM((row_tiles, width, tile), BF16),
            pltpu.VMEM((col_tiles, width, tile), BF16),
            pltpu.VMEM((slots + 1, width, tile), F32),
            pltpu.VMEM((slots + 1, width, tile), F32),
            pltpu.VMEM((2, *wire_u), BF16),
            pltpu.VMEM((2, *wire_i), BF16),
            pltpu.VMEM((2, n_item, *wire_u), BF16),
            pltpu.VMEM((2, n_user, *wire_i), BF16),
            pltpu.VMEM((2, n_item, *wire_u), sent),
            pltpu.VMEM((2, n_user, *wire_i), sent),
            pltpu.VMEM((2, n_item, *wire_u), sent),
            pltpu.VMEM((2, n_user, *wire_i), sent),
            dma((slots,)), dma((7,)),
            dma((2, n_item)), dma((2, n_item)), dma((2, n_user)), dma((2, n_user)),
            dma((2, n_item)), dma((2, n_item)), dma((2, n_user)), dma((2, n_user)),
        ],
        compiler_params=pltpu.CompilerParams(
            collective_id=0, has_side_effects=True, vmem_limit_bytes=62 * 1024 * 1024
        ),
    )(
        user_cot.T, item_cot.T, tile_weight, tile_rows, tile_cols, tile_count,
        user_degree, item_degree,
    )
    return user_grad.T, item_grad.T


def solution(mesh):
    return jax.shard_map(
        functools.partial(shards, mesh.shape["user"], mesh.shape["item"]),
        mesh=mesh,
        in_specs=(
            P(("user", "item"), None),
            P(("item", "user"), None),
            P("user", "item", None),
            P("user", "item"),
            P("user", "item"),
            P("user", "item"),
            P("user"),
            P("item"),
        ),
        out_specs=(P(("user", "item"), None), P(("item", "user"), None)),
        check_vma=False,
    )
```

```python
import functools
import math

import jax
import jax.numpy as jnp
from jax import lax
from jax.experimental import pallas as pl
from jax.experimental.pallas import tpu as pltpu
from jax.sharding import PartitionSpec as P

F32 = jnp.float32
BF16 = jnp.bfloat16
MESH = pl.DeviceIdType.MESH


def kernel(
    sizes, user_cot, item_cot, weight, rows_in, cols_in, count_in, user_deg, item_deg,
    user_grad, item_grad,
    cot_u, cot_i, deg_u, deg_i, rows, cols, count,
    raw, adj, row_scale, col_scale, user_panel, item_panel, to_user, to_item,
    user_pack, item_pack,
    ag_user, ag_item, out_user, out_item, in_user, in_item,
    load_sem, small_sem, ag_send_u, ag_recv_u, ag_send_i, ag_recv_i, rs_send_u, rs_recv_u, rs_send_i, rs_recv_i,
):
    n_user, n_item, slots, tile, width, row_tiles, col_tiles = sizes
    me_u, me_i = lax.axis_index("user"), lax.axis_index("item")
    piece_u, piece_i = cot_u.shape[1], cot_i.shape[1]

    small = [
        pltpu.make_async_copy(src, dst, small_sem.at[j])
        for j, (src, dst) in enumerate([
            (user_cot, cot_u), (item_cot, cot_i), (user_deg, deg_u), (item_deg, deg_i),
            (rows_in, rows), (cols_in, cols), (count_in, count),
        ])
    ]
    for copy in small:
        copy.start()
    for t in range(slots):
        pltpu.make_async_copy(weight.at[t], raw.at[t], load_sem.at[t]).start()

    barrier = pltpu.get_barrier_semaphore()

    def greet(axis, me, n):
        def step(k, carry):
            pl.semaphore_signal(
                barrier, inc=1, device_id={axis: lax.rem(me + k, n)}, device_id_type=MESH
            )
            return carry
        if n > 8:
            lax.fori_loop(1, n, step, 0)
        else:
            for k in range(1, n):
                step(k, 0)

    greet("item", me_i, n_item)
    greet("user", me_u, n_user)

    grain = math.gcd(piece_u, 128)
    folds, whole_lanes = 128 // grain, piece_u // 128 * 128
    fold_rows, main_rows = width // folds, width * (piece_u // 128)

    def fold_in(put, take):
        for j in range(0, whole_lanes, 128):
            put(j // 128 * width, take(j, 128))
        if whole_lanes < piece_u:
            rest = take(whole_lanes, grain)
            put(main_rows, jnp.concatenate(
                [rest[f * fold_rows : (f + 1) * fold_rows, :] for f in range(folds)], axis=1))

    def unfold(wire, lane, size):
        if lane < whole_lanes:
            at = lane // 128 * width
            return wire[at : at + width, lane % 128 : lane % 128 + size]
        rest = wire[main_rows : main_rows + fold_rows, :]
        return jnp.concatenate(
            [rest[:, f * grain : (f + 1) * grain] for f in range(folds)], axis=0)

    for copy in small[:2]:
        copy.wait()
    own = cot_u[...]

    def put_own(at, value):
        user_pack[0, at : at + value.shape[0], :] = value

    fold_in(put_own, lambda lane, size: own[:, lane : lane + size])
    item_pack[0] = cot_i[...]
    ag_user[0, me_i] = user_pack[0]
    ag_item[0, me_u] = item_pack[0]

    pl.semaphore_wait(barrier, n_user + n_item - 2)

    def gather_copy(axis, me, n, buf, send, recv, hop, k):
        there = lax.rem(me + k, n)
        return pltpu.make_async_remote_copy(
            src_ref=buf.at[hop, me], dst_ref=buf.at[hop, me],
            send_sem=send.at[hop], recv_sem=recv.at[hop],
            device_id={axis: there}, device_id_type=MESH,
        )

    def settle_copy(axis, me, n, src, dst, send, recv, hop, k):
        there = lax.rem(me + k, n)
        return pltpu.make_async_remote_copy(
            src_ref=src.at[hop, there], dst_ref=dst.at[hop, me],
            send_sem=send.at[hop], recv_sem=recv.at[hop],
            device_id={axis: there}, device_id_type=MESH,
        )

    def all_of(axis, me, n, src, dst, send, recv, hop):
        return pltpu.make_async_remote_copy(
            src_ref=src.at[hop, pl.ds(0, n - 1)], dst_ref=dst.at[hop, pl.ds(0, n - 1)],
            send_sem=send.at[hop], recv_sem=recv.at[hop],
            device_id={axis: lax.rem(me + 1, n)}, device_id_type=MESH,
        )

    AG_U = ("item", me_i, n_item, ag_user, ag_send_u, ag_recv_u)
    AG_I = ("user", me_u, n_user, ag_item, ag_send_i, ag_recv_i)
    RS_U = ("item", me_i, n_item, out_user, in_user, rs_send_u, rs_recv_u)
    RS_I = ("user", me_u, n_user, out_item, in_item, rs_send_i, rs_recv_i)

    def each(n, fn):
        def step(k, carry):
            fn(k)
            return carry
        if n > 8:
            lax.fori_loop(1, n, step, 0)
        else:
            for k in range(1, n):
                fn(k)

    def start_gather(g, hop):
        each(g[2], lambda k: gather_copy(*g, hop, k).start())

    def end_gather(g, hop):
        all_of(*g[:4], *g[3:], hop).wait_recv()

    def start_settle(s, hop):
        each(s[2], lambda k: settle_copy(*s, hop, k).start())

    def end_settle(s, hop):
        all_of(*s, hop).wait_recv()

    start_gather(AG_U, 0)
    start_gather(AG_I, 0)

    for copy in small[2:]:
        copy.wait()
    for r in range(row_tiles):
        scale = lax.rsqrt(deg_u[r * tile : (r + 1) * tile].astype(F32)).reshape(1, tile)
        row_scale[r] = jnp.transpose(jnp.broadcast_to(scale, (128, tile)))
    for c in range(col_tiles):
        col_scale[c] = lax.rsqrt(deg_i[c * tile : (c + 1) * tile].astype(F32)).reshape(1, tile)
    row_id = [rows[0, t] for t in range(slots)]
    col_id = [cols[0, t] for t in range(slots)]

    def chain(ids, blocks):
        before = []
        for t in range(slots):
            prev = jnp.int32(slots)
            for s in range(t):
                prev = jnp.where(ids[s] == ids[t], jnp.int32(s), prev)
            before.append(prev)
        last = []
        for b in range(blocks):
            found = jnp.int32(slots)
            for t in range(slots):
                found = jnp.where(ids[t] == b, jnp.int32(t), found)
            last.append(found)
        return before, last

    row_before, row_last = chain(row_id, row_tiles)
    col_before, col_last = chain(col_id, col_tiles)
    to_user[slots] = jnp.zeros((width, tile), F32)
    to_item[slots] = jnp.zeros((width, tile), F32)
    live = count[0, 0]
    for t in range(slots):
        pltpu.make_async_copy(weight.at[t], raw.at[t], load_sem.at[t]).wait()
        on = jnp.where(t < live, jnp.float32(1), jnp.float32(0))
        rs = row_scale[row_id[t]]
        cs = col_scale[col_id[t]] * on
        w = raw[t].astype(F32)
        a = jnp.concatenate(
            [(w[:, j : j + 128] * rs) * cs[:, j : j + 128] for j in range(0, tile, 128)], axis=1
        ).astype(BF16)
        adj[t] = a

    def user_terms(hop):
        end_gather(AG_I, hop)
        for p in range(n_user):
            for lane in range(0, piece_i, 128):
                b, off = divmod(p * piece_i + lane, tile)
                item_panel[b, :, off : off + 128] = ag_item[hop, p, :, lane : lane + 128]
        for t in range(slots):
            to_user[t] = to_user[row_before[t]] + lax.dot_general(
                item_panel[col_id[t]], adj[t], (((1,), (1,)), ((), ())),
                preferred_element_type=F32,
            )
        tiles = [to_user[row_last[r]].astype(out_user.dtype) for r in range(row_tiles)]

        def lanes(at, size):
            parts = []
            while size:
                b, off = divmod(at, tile)
                step = size if off % 128 == 0 and off + size <= tile else grain
                parts.append(tiles[b][:, off : off + step])
                at, size = at + step, size - step
            return parts[0] if len(parts) == 1 else jnp.concatenate(parts, axis=1)

        for p in range(n_item):
            def put(at, value):
                out_user[hop, p, at : at + value.shape[0], :] = value

            fold_in(put, lambda lane, size: lanes(p * piece_u + lane, size))
        in_user[hop, me_i] = out_user[hop, me_i]
        start_settle(RS_U, hop)

    def item_terms(hop):
        end_gather(AG_U, hop)
        wires = [ag_user[hop, p] for p in range(n_item)]
        for at in range(0, n_item * piece_u, 128):
            p, lane = divmod(at, piece_u)
            if lane % 128 == 0 and lane < whole_lanes:
                block = unfold(wires[p], lane, 128)
            else:
                parts = []
                for g in range(at, at + 128, grain):
                    p, lane = divmod(g, piece_u)
                    parts.append(unfold(wires[p], lane, grain))
                block = jnp.concatenate(parts, axis=1)
            b, off = divmod(at, tile)
            user_panel[b, :, off : off + 128] = block
        for t in range(slots):
            to_item[t] = to_item[col_before[t]] + jnp.dot(
                user_panel[row_id[t]], adj[t], preferred_element_type=F32
            )
        for c in range(col_tiles):
            done = to_item[col_last[c]].astype(out_item.dtype)
            for lane in range(0, tile, 128):
                p, off = divmod(c * tile + lane, piece_i)
                out_item[hop, p, :, off : off + 128] = done[:, lane : lane + 128]
        in_item[hop, me_u] = out_item[hop, me_u]
        start_settle(RS_I, hop)

    def total(s, hop):
        end_settle(s, hop)
        dst = s[4]
        acc = dst[hop, 0].astype(F32)
        for p in range(1, s[2]):
            acc = acc + dst[hop, p].astype(F32)
        return acc

    user_terms(0)
    item_terms(0)
    once_i = total(RS_I, 0).astype(BF16)
    ag_item[1, me_u] = once_i
    start_gather(AG_I, 1)
    item_pack[1] = once_i
    once_u = total(RS_U, 0).astype(BF16)
    ag_user[1, me_i] = once_u
    start_gather(AG_U, 1)
    user_pack[1] = once_u
    user_terms(1)
    item_terms(1)

    def finish(s, packed):
        twice = total(s, 1)
        return ((packed[0].astype(F32) + packed[1].astype(F32) + twice) / 3.0).astype(BF16)

    item_grad[...] = finish(RS_I, item_pack)
    wire = finish(RS_U, user_pack)
    for lane in range(0, whole_lanes, 128):
        user_grad[:, lane : lane + 128] = unfold(wire, lane, 128)
    if whole_lanes < piece_u:
        user_grad[:, whole_lanes:piece_u] = unfold(wire, whole_lanes, grain)

    for hop in range(2):
        for g in (AG_U, AG_I):
            all_of(*g[:4], *g[3:], hop).wait_send()
        for s in (RS_U, RS_I):
            all_of(*s, hop).wait_send()


def shards(n_user, n_item, user_cot, item_cot, tile_weight, tile_rows, tile_cols, tile_count, user_degree, item_degree):
    slots, tile = tile_weight.shape[0], tile_weight.shape[2]
    width = user_cot.shape[1]
    shard_users, shard_items = user_degree.shape[0], item_degree.shape[0]
    row_tiles, col_tiles = shard_users // tile, shard_items // tile
    piece_u, piece_i = user_cot.shape[0], item_cot.shape[0]
    wire_u = (width * piece_u // 128, 128)
    wire_i = (width, piece_i)
    sizes = (n_user, n_item, slots, tile, width, row_tiles, col_tiles)
    sent = BF16
    vmem = pl.BlockSpec(memory_space=pltpu.VMEM)
    dma = pltpu.SemaphoreType.DMA
    user_grad, item_grad = pl.pallas_call(
        functools.partial(kernel, sizes),
        out_shape=(
            jax.ShapeDtypeStruct((width, piece_u), BF16),
            jax.ShapeDtypeStruct((width, piece_i), BF16),
        ),
        in_specs=[pl.BlockSpec(memory_space=pl.ANY)] * 8,
        out_specs=(vmem, vmem),
        scratch_shapes=[
            pltpu.VMEM((width, piece_u), BF16),
            pltpu.VMEM((width, piece_i), BF16),
            pltpu.VMEM((shard_users,), jnp.int32),
            pltpu.VMEM((shard_items,), jnp.int32),
            pltpu.SMEM(tile_rows.shape, jnp.int32),
            pltpu.SMEM(tile_cols.shape, jnp.int32),
            pltpu.SMEM(tile_count.shape, jnp.int32),
            pltpu.VMEM((slots, tile, tile), jnp.int32),
            pltpu.VMEM((slots, tile, tile), BF16),
            pltpu.VMEM((row_tiles, tile, 128), F32),
            pltpu.VMEM((col_tiles, 1, tile), F32),
            pltpu.VMEM((row_tiles, width, tile), BF16),
            pltpu.VMEM((col_tiles, width, tile), BF16),
            pltpu.VMEM((slots + 1, width, tile), F32),
            pltpu.VMEM((slots + 1, width, tile), F32),
            pltpu.VMEM((2, *wire_u), BF16),
            pltpu.VMEM((2, *wire_i), BF16),
            pltpu.VMEM((2, n_item, *wire_u), BF16),
            pltpu.VMEM((2, n_user, *wire_i), BF16),
            pltpu.VMEM((2, n_item, *wire_u), sent),
            pltpu.VMEM((2, n_user, *wire_i), sent),
            pltpu.VMEM((2, n_item, *wire_u), sent),
            pltpu.VMEM((2, n_user, *wire_i), sent),
            dma((slots,)), dma((7,)),
            *[dma((2,))] * 8,
        ],
        compiler_params=pltpu.CompilerParams(
            collective_id=0, has_side_effects=True, vmem_limit_bytes=62 * 1024 * 1024
        ),
    )(
        user_cot.T, item_cot.T, tile_weight, tile_rows, tile_cols, tile_count,
        user_degree, item_degree,
    )
    return user_grad.T, item_grad.T


def solution(mesh):
    return jax.shard_map(
        functools.partial(shards, mesh.shape["user"], mesh.shape["item"]),
        mesh=mesh,
        in_specs=(
            P(("user", "item"), None),
            P(("item", "user"), None),
            P("user", "item", None),
            P("user", "item"),
            P("user", "item"),
            P("user", "item"),
            P("user"),
            P("item"),
        ),
        out_specs=(P(("user", "item"), None), P(("item", "user"), None)),
        check_vma=False,
    )
```

```python
import functools
import math

import jax
import jax.numpy as jnp
from jax import lax
from jax.experimental import pallas as pl
from jax.experimental.pallas import tpu as pltpu
from jax.sharding import PartitionSpec as P

F32 = jnp.float32
BF16 = jnp.bfloat16
MESH = pl.DeviceIdType.MESH


def kernel(
    sizes, user_cot, item_cot, weight, rows_in, cols_in, count_in, user_deg, item_deg,
    user_grad, item_grad,
    cot_u, cot_i, deg_u, deg_i, rows, cols, count,
    raw, adj, row_scale, col_scale, user_panel, item_panel, to_user, to_item,
    user_pack, item_pack,
    ag_user, ag_item, out_user, out_item, in_user, in_item,
    load_sem, small_sem, ag_send_u, ag_recv_u, ag_send_i, ag_recv_i, rs_send_u, rs_recv_u, rs_send_i, rs_recv_i,
):
    n_user, n_item, slots, tile, width, row_tiles, col_tiles = sizes
    me_u, me_i = lax.axis_index("user"), lax.axis_index("item")
    piece_u, piece_i = cot_u.shape[1], cot_i.shape[1]

    small = [
        pltpu.make_async_copy(src, dst, small_sem.at[j])
        for j, (src, dst) in enumerate([
            (user_cot, cot_u), (item_cot, cot_i), (user_deg, deg_u), (item_deg, deg_i),
            (rows_in, rows), (cols_in, cols), (count_in, count),
        ])
    ]
    for copy in small[:2]:
        copy.start()
    barrier = pltpu.get_barrier_semaphore()

    def greet(axis, me, n):
        def step(k, carry):
            pl.semaphore_signal(
                barrier, inc=1, device_id={axis: lax.rem(me + k, n)}, device_id_type=MESH
            )
            return carry
        if n > 8:
            lax.fori_loop(1, n, step, 0)
        else:
            for k in range(1, n):
                step(k, 0)

    greet("item", me_i, n_item)
    greet("user", me_u, n_user)
    for copy in small[2:]:
        copy.start()
    for t in range(slots):
        pltpu.make_async_copy(weight.at[t], raw.at[t], load_sem.at[t]).start()


    grain = math.gcd(piece_u, 128)
    folds, whole_lanes = 128 // grain, piece_u // 128 * 128
    fold_rows, main_rows = width // folds, width * (piece_u // 128)

    def fold_in(put, take):
        for j in range(0, whole_lanes, 128):
            put(j // 128 * width, take(j, 128))
        if whole_lanes < piece_u:
            rest = take(whole_lanes, grain)
            put(main_rows, jnp.concatenate(
                [rest[f * fold_rows : (f + 1) * fold_rows, :] for f in range(folds)], axis=1))

    def unfold(wire, lane, size):
        if lane < whole_lanes:
            at = lane // 128 * width
            return wire[at : at + width, lane % 128 : lane % 128 + size]
        rest = wire[main_rows : main_rows + fold_rows, :]
        return jnp.concatenate(
            [rest[:, f * grain : (f + 1) * grain] for f in range(folds)], axis=0)

    for copy in small[:2]:
        copy.wait()
    own = cot_u[...]

    def put_own(at, value):
        user_pack[0, at : at + value.shape[0], :] = value

    fold_in(put_own, lambda lane, size: own[:, lane : lane + size])
    item_pack[0] = cot_i[...]
    ag_user[0, me_i] = user_pack[0]
    ag_item[0, me_u] = item_pack[0]

    pl.semaphore_wait(barrier, n_user + n_item - 2)

    def gather_copy(axis, me, n, buf, send, recv, hop, k):
        there = lax.rem(me + k, n)
        return pltpu.make_async_remote_copy(
            src_ref=buf.at[hop, me], dst_ref=buf.at[hop, me],
            send_sem=send.at[hop], recv_sem=recv.at[hop],
            device_id={axis: there}, device_id_type=MESH,
        )

    def settle_copy(axis, me, n, src, dst, send, recv, hop, k):
        there = lax.rem(me + k, n)
        return pltpu.make_async_remote_copy(
            src_ref=src.at[hop, there], dst_ref=dst.at[hop, me],
            send_sem=send.at[hop], recv_sem=recv.at[hop],
            device_id={axis: there}, device_id_type=MESH,
        )

    def all_of(axis, me, n, src, dst, send, recv, hop):
        return pltpu.make_async_remote_copy(
            src_ref=src.at[hop, pl.ds(0, n - 1)], dst_ref=dst.at[hop, pl.ds(0, n - 1)],
            send_sem=send.at[hop], recv_sem=recv.at[hop],
            device_id={axis: lax.rem(me + 1, n)}, device_id_type=MESH,
        )

    AG_U = ("item", me_i, n_item, ag_user, ag_send_u, ag_recv_u)
    AG_I = ("user", me_u, n_user, ag_item, ag_send_i, ag_recv_i)
    RS_U = ("item", me_i, n_item, out_user, in_user, rs_send_u, rs_recv_u)
    RS_I = ("user", me_u, n_user, out_item, in_item, rs_send_i, rs_recv_i)

    def each(n, fn):
        def step(k, carry):
            fn(k)
            return carry
        if n > 8:
            lax.fori_loop(1, n, step, 0)
        else:
            for k in range(1, n):
                fn(k)

    def start_gather(g, hop):
        each(g[2], lambda k: gather_copy(*g, hop, k).start())

    def end_gather(g, hop):
        all_of(*g[:4], *g[3:], hop).wait_recv()

    def start_settle(s, hop):
        each(s[2], lambda k: settle_copy(*s, hop, k).start())

    def end_settle(s, hop):
        all_of(*s, hop).wait_recv()

    start_gather(AG_I, 0)
    start_gather(AG_U, 0)

    for copy in small[2:]:
        copy.wait()
    for r in range(row_tiles):
        scale = lax.rsqrt(deg_u[r * tile : (r + 1) * tile].astype(F32)).reshape(1, tile)
        row_scale[r] = jnp.transpose(jnp.broadcast_to(scale, (128, tile)))
    for c in range(col_tiles):
        col_scale[c] = lax.rsqrt(deg_i[c * tile : (c + 1) * tile].astype(F32)).reshape(1, tile)
    row_id = [rows[0, t] for t in range(slots)]
    col_id = [cols[0, t] for t in range(slots)]

    def chain(ids, blocks):
        before = []
        for t in range(slots):
            prev = jnp.int32(slots)
            for s in range(t):
                prev = jnp.where(ids[s] == ids[t], jnp.int32(s), prev)
            before.append(prev)
        last = []
        for b in range(blocks):
            found = jnp.int32(slots)
            for t in range(slots):
                found = jnp.where(ids[t] == b, jnp.int32(t), found)
            last.append(found)
        return before, last

    row_before, row_last = chain(row_id, row_tiles)
    col_before, col_last = chain(col_id, col_tiles)
    to_user[slots] = jnp.zeros((width, tile), F32)
    to_item[slots] = jnp.zeros((width, tile), F32)
    live = count[0, 0]
    for t in range(slots):
        pltpu.make_async_copy(weight.at[t], raw.at[t], load_sem.at[t]).wait()
        on = jnp.where(t < live, jnp.float32(1), jnp.float32(0))
        rs = row_scale[row_id[t]]
        cs = col_scale[col_id[t]] * on
        w = raw[t].astype(F32)
        a = jnp.concatenate(
            [(w[:, j : j + 128] * rs) * cs[:, j : j + 128] for j in range(0, tile, 128)], axis=1
        ).astype(BF16)
        adj[t] = a

    def user_terms(hop):
        end_gather(AG_I, hop)
        for p in range(n_user):
            for lane in range(0, piece_i, 128):
                b, off = divmod(p * piece_i + lane, tile)
                item_panel[b, :, off : off + 128] = ag_item[hop, p, :, lane : lane + 128]
        for t in range(slots):
            to_user[t] = to_user[row_before[t]] + lax.dot_general(
                item_panel[col_id[t]], adj[t], (((1,), (1,)), ((), ())),
                preferred_element_type=F32,
            )
        tiles = [to_user[row_last[r]].astype(out_user.dtype) for r in range(row_tiles)]

        def lanes(at, size):
            parts = []
            while size:
                b, off = divmod(at, tile)
                step = size if off % 128 == 0 and off + size <= tile else grain
                parts.append(tiles[b][:, off : off + step])
                at, size = at + step, size - step
            return parts[0] if len(parts) == 1 else jnp.concatenate(parts, axis=1)

        for p in range(n_item):
            def put(at, value):
                out_user[hop, p, at : at + value.shape[0], :] = value

            fold_in(put, lambda lane, size: lanes(p * piece_u + lane, size))
        start_settle(RS_U, hop)
        in_user[hop, me_i] = out_user[hop, me_i]

    def item_terms(hop):
        end_gather(AG_U, hop)
        wires = [ag_user[hop, p] for p in range(n_item)]
        for at in range(0, n_item * piece_u, 128):
            p, lane = divmod(at, piece_u)
            if lane % 128 == 0 and lane < whole_lanes:
                block = unfold(wires[p], lane, 128)
            else:
                parts = []
                for g in range(at, at + 128, grain):
                    p, lane = divmod(g, piece_u)
                    parts.append(unfold(wires[p], lane, grain))
                block = jnp.concatenate(parts, axis=1)
            b, off = divmod(at, tile)
            user_panel[b, :, off : off + 128] = block
        for t in range(slots):
            to_item[t] = to_item[col_before[t]] + jnp.dot(
                user_panel[row_id[t]], adj[t], preferred_element_type=F32
            )
        for c in range(col_tiles):
            done = to_item[col_last[c]].astype(out_item.dtype)
            for lane in range(0, tile, 128):
                p, off = divmod(c * tile + lane, piece_i)
                out_item[hop, p, :, off : off + 128] = done[:, lane : lane + 128]
        start_settle(RS_I, hop)
        in_item[hop, me_u] = out_item[hop, me_u]

    def total(s, hop):
        end_settle(s, hop)
        dst = s[4]
        acc = dst[hop, 0].astype(F32)
        for p in range(1, s[2]):
            acc = acc + dst[hop, p].astype(F32)
        return acc

    user_terms(0)
    item_terms(0)
    once_i = total(RS_I, 0).astype(BF16)
    ag_item[1, me_u] = once_i
    start_gather(AG_I, 1)
    item_pack[1] = once_i
    once_u = total(RS_U, 0).astype(BF16)
    ag_user[1, me_i] = once_u
    start_gather(AG_U, 1)
    user_pack[1] = once_u
    user_terms(1)
    item_terms(1)

    def finish(s, packed):
        twice = total(s, 1)
        return ((packed[0].astype(F32) + packed[1].astype(F32) + twice) / 3.0).astype(BF16)

    item_grad[...] = finish(RS_I, item_pack)
    wire = finish(RS_U, user_pack)
    for lane in range(0, whole_lanes, 128):
        user_grad[:, lane : lane + 128] = unfold(wire, lane, 128)
    if whole_lanes < piece_u:
        user_grad[:, whole_lanes:piece_u] = unfold(wire, whole_lanes, grain)

    for hop in range(2):
        for g in (AG_U, AG_I):
            all_of(*g[:4], *g[3:], hop).wait_send()
        for s in (RS_U, RS_I):
            all_of(*s, hop).wait_send()


def shards(n_user, n_item, user_cot, item_cot, tile_weight, tile_rows, tile_cols, tile_count, user_degree, item_degree):
    slots, tile = tile_weight.shape[0], tile_weight.shape[2]
    width = user_cot.shape[1]
    shard_users, shard_items = user_degree.shape[0], item_degree.shape[0]
    row_tiles, col_tiles = shard_users // tile, shard_items // tile
    piece_u, piece_i = user_cot.shape[0], item_cot.shape[0]
    wire_u = (width * piece_u // 128, 128)
    wire_i = (width, piece_i)
    sizes = (n_user, n_item, slots, tile, width, row_tiles, col_tiles)
    sent = BF16
    vmem = pl.BlockSpec(memory_space=pltpu.VMEM)
    dma = pltpu.SemaphoreType.DMA
    user_grad, item_grad = pl.pallas_call(
        functools.partial(kernel, sizes),
        out_shape=(
            pltpu.VMEM((width, piece_u), BF16),
            pltpu.VMEM((width, piece_i), BF16),
        ),
        in_specs=[pl.BlockSpec(memory_space=pl.ANY)] * 8,
        out_specs=(vmem, vmem),
        scratch_shapes=[
            pltpu.VMEM((width, piece_u), BF16),
            pltpu.VMEM((width, piece_i), BF16),
            pltpu.VMEM((shard_users,), jnp.int32),
            pltpu.VMEM((shard_items,), jnp.int32),
            pltpu.SMEM(tile_rows.shape, jnp.int32),
            pltpu.SMEM(tile_cols.shape, jnp.int32),
            pltpu.SMEM(tile_count.shape, jnp.int32),
            pltpu.VMEM((slots, tile, tile), jnp.int32),
            pltpu.VMEM((slots, tile, tile), BF16),
            pltpu.VMEM((row_tiles, tile, 128), F32),
            pltpu.VMEM((col_tiles, 1, tile), F32),
            pltpu.VMEM((row_tiles, width, tile), BF16),
            pltpu.VMEM((col_tiles, width, tile), BF16),
            pltpu.VMEM((slots + 1, width, tile), F32),
            pltpu.VMEM((slots + 1, width, tile), F32),
            pltpu.VMEM((2, *wire_u), BF16),
            pltpu.VMEM((2, *wire_i), BF16),
            pltpu.VMEM((2, n_item, *wire_u), BF16),
            pltpu.VMEM((2, n_user, *wire_i), BF16),
            pltpu.VMEM((2, n_item, *wire_u), sent),
            pltpu.VMEM((2, n_user, *wire_i), sent),
            pltpu.VMEM((2, n_item, *wire_u), sent),
            pltpu.VMEM((2, n_user, *wire_i), sent),
            dma((slots,)), dma((7,)),
            *[dma((2,))] * 8,
        ],
        compiler_params=pltpu.CompilerParams(
            collective_id=0, has_side_effects=True, vmem_limit_bytes=60 * 1024 * 1024
        ),
    )(
        user_cot.T, item_cot.T, tile_weight, tile_rows, tile_cols, tile_count,
        user_degree, item_degree,
    )
    return user_grad.T, item_grad.T


def solution(mesh):
    return jax.shard_map(
        functools.partial(shards, mesh.shape["user"], mesh.shape["item"]),
        mesh=mesh,
        in_specs=(
            P(("user", "item"), None),
            P(("item", "user"), None),
            P("user", "item", None),
            P("user", "item"),
            P("user", "item"),
            P("user", "item"),
            P("user"),
            P("item"),
        ),
        out_specs=(P(("user", "item"), None), P(("item", "user"), None)),
        check_vma=False,
    )
```

```python
import functools
import math

import jax
import jax.numpy as jnp
from jax import lax
from jax.experimental import pallas as pl
from jax.experimental.pallas import tpu as pltpu
from jax.sharding import PartitionSpec as P

F32 = jnp.float32
BF16 = jnp.bfloat16
MESH = pl.DeviceIdType.MESH


def kernel(
    sizes, user_cot, item_cot, weight, rows_in, cols_in, count_in, user_deg, item_deg,
    user_grad, item_grad,
    cot_u, cot_i, deg_u, deg_i, rows, cols, count,
    raw, adj, row_scale, col_scale, user_panel, item_panel, to_user, to_item,
    user_pack, item_pack,
    ag_user, ag_item, out_user, out_item, in_user, in_item,
    load_sem, small_sem, ag_send_u, ag_recv_u, ag_send_i, ag_recv_i, rs_send_u, rs_recv_u, rs_send_i, rs_recv_i,
):
    n_user, n_item, slots, tile, width, row_tiles, col_tiles = sizes
    me_u, me_i = lax.axis_index("user"), lax.axis_index("item")
    piece_u, piece_i = cot_u.shape[1], cot_i.shape[1]

    small = [
        pltpu.make_async_copy(src, dst, small_sem.at[j])
        for j, (src, dst) in enumerate([
            (user_cot, cot_u), (item_cot, cot_i), (user_deg, deg_u), (item_deg, deg_i),
            (rows_in, rows), (cols_in, cols), (count_in, count),
        ])
    ]
    for copy in small[:2]:
        copy.start()
    barrier = pltpu.get_barrier_semaphore()

    def greet(axis, me, n):
        def step(k, carry):
            pl.semaphore_signal(
                barrier, inc=1, device_id={axis: lax.rem(me + k, n)}, device_id_type=MESH
            )
            return carry
        if n > 8:
            lax.fori_loop(1, n, step, 0)
        else:
            for k in range(1, n):
                step(k, 0)

    greet("item", me_i, n_item)
    greet("user", me_u, n_user)
    for copy in small[2:]:
        copy.start()
    for t in range(slots):
        pltpu.make_async_copy(weight.at[t], raw.at[t], load_sem.at[t]).start()


    grain = math.gcd(piece_u, 128)
    folds, whole_lanes = 128 // grain, piece_u // 128 * 128
    fold_rows, main_rows = width // folds, width * (piece_u // 128)

    def fold_in(put, take):
        for j in range(0, whole_lanes, 128):
            put(j // 128 * width, take(j, 128))
        if whole_lanes < piece_u:
            rest = take(whole_lanes, grain)
            put(main_rows, jnp.concatenate(
                [rest[f * fold_rows : (f + 1) * fold_rows, :] for f in range(folds)], axis=1))

    def unfold(wire, lane, size):
        if lane < whole_lanes:
            at = lane // 128 * width
            return wire[at : at + width, lane % 128 : lane % 128 + size]
        rest = wire[main_rows : main_rows + fold_rows, :]
        return jnp.concatenate(
            [rest[:, f * grain : (f + 1) * grain] for f in range(folds)], axis=0)

    for copy in small[:2]:
        copy.wait()
    own = cot_u[...]

    def put_own(at, value):
        user_pack[0, at : at + value.shape[0], :] = value

    fold_in(put_own, lambda lane, size: own[:, lane : lane + size])
    item_pack[0] = cot_i[...]
    ag_user[0, me_i] = user_pack[0]
    ag_item[0, me_u] = item_pack[0]

    pl.semaphore_wait(barrier, n_user + n_item - 2)

    def gather_copy(axis, me, n, buf, send, recv, hop, k):
        there = lax.rem(me + k, n)
        return pltpu.make_async_remote_copy(
            src_ref=buf.at[hop, me], dst_ref=buf.at[hop, me],
            send_sem=send.at[hop], recv_sem=recv.at[hop],
            device_id={axis: there}, device_id_type=MESH,
        )

    def settle_copy(axis, me, n, src, dst, send, recv, hop, k):
        there = lax.rem(me + k, n)
        return pltpu.make_async_remote_copy(
            src_ref=src.at[hop, there], dst_ref=dst.at[hop, me],
            send_sem=send.at[hop], recv_sem=recv.at[hop],
            device_id={axis: there}, device_id_type=MESH,
        )

    def all_of(axis, me, n, src, dst, send, recv, hop):
        return pltpu.make_async_remote_copy(
            src_ref=src.at[hop, pl.ds(0, n - 1)], dst_ref=dst.at[hop, pl.ds(0, n - 1)],
            send_sem=send.at[hop], recv_sem=recv.at[hop],
            device_id={axis: lax.rem(me + 1, n)}, device_id_type=MESH,
        )

    AG_U = ("item", me_i, n_item, ag_user, ag_send_u, ag_recv_u)
    AG_I = ("user", me_u, n_user, ag_item, ag_send_i, ag_recv_i)
    RS_U = ("item", me_i, n_item, out_user, in_user, rs_send_u, rs_recv_u)
    RS_I = ("user", me_u, n_user, out_item, in_item, rs_send_i, rs_recv_i)

    def each(n, fn):
        def step(k, carry):
            fn(k)
            return carry
        if n > 8:
            lax.fori_loop(1, n, step, 0)
        else:
            for k in range(1, n):
                fn(k)

    def start_gather(g, hop):
        each(g[2], lambda k: gather_copy(*g, hop, k).start())

    def end_gather(g, hop):
        all_of(*g[:4], *g[3:], hop).wait_recv()

    def start_settle(s, hop):
        each(s[2], lambda k: settle_copy(*s, hop, k).start())

    def send_now(s, hop, p):
        axis, me, n, src, dst, send, recv = s

        @pl.when(p != me)
        def _():
            pltpu.make_async_remote_copy(
                src_ref=src.at[hop, p], dst_ref=dst.at[hop, me],
                send_sem=send.at[hop], recv_sem=recv.at[hop],
                device_id={axis: jnp.int32(p)}, device_id_type=MESH,
            ).start()

    def end_settle(s, hop):
        all_of(*s, hop).wait_recv()

    start_gather(AG_I, 0)
    start_gather(AG_U, 0)

    for copy in small[2:]:
        copy.wait()
    for r in range(row_tiles):
        scale = lax.rsqrt(deg_u[r * tile : (r + 1) * tile].astype(F32)).reshape(1, tile)
        row_scale[r] = jnp.transpose(jnp.broadcast_to(scale, (128, tile)))
    for c in range(col_tiles):
        col_scale[c] = lax.rsqrt(deg_i[c * tile : (c + 1) * tile].astype(F32)).reshape(1, tile)
    row_id = [rows[0, t] for t in range(slots)]
    col_id = [cols[0, t] for t in range(slots)]

    def chain(ids, blocks):
        before = []
        for t in range(slots):
            prev = jnp.int32(slots)
            for s in range(t):
                prev = jnp.where(ids[s] == ids[t], jnp.int32(s), prev)
            before.append(prev)
        last = []
        for b in range(blocks):
            found = jnp.int32(slots)
            for t in range(slots):
                found = jnp.where(ids[t] == b, jnp.int32(t), found)
            last.append(found)
        return before, last

    row_before, row_last = chain(row_id, row_tiles)
    col_before, col_last = chain(col_id, col_tiles)
    to_user[slots] = jnp.zeros((width, tile), F32)
    to_item[slots] = jnp.zeros((width, tile), F32)
    live = count[0, 0]
    for t in range(slots):
        pltpu.make_async_copy(weight.at[t], raw.at[t], load_sem.at[t]).wait()
        on = jnp.where(t < live, jnp.float32(1), jnp.float32(0))
        rs = row_scale[row_id[t]]
        cs = col_scale[col_id[t]] * on
        w = raw[t].astype(F32)
        a = jnp.concatenate(
            [(w[:, j : j + 128] * rs) * cs[:, j : j + 128] for j in range(0, tile, 128)], axis=1
        ).astype(BF16)
        adj[t] = a

    def user_terms(hop):
        end_gather(AG_I, hop)
        for p in range(n_user):
            for lane in range(0, piece_i, 128):
                b, off = divmod(p * piece_i + lane, tile)
                item_panel[b, :, off : off + 128] = ag_item[hop, p, :, lane : lane + 128]
        for t in range(slots):
            to_user[t] = to_user[row_before[t]] + lax.dot_general(
                item_panel[col_id[t]], adj[t], (((1,), (1,)), ((), ())),
                preferred_element_type=F32,
            )
        tiles = [to_user[row_last[r]].astype(out_user.dtype) for r in range(row_tiles)]

        def lanes(at, size):
            parts = []
            while size:
                b, off = divmod(at, tile)
                step = size if off % 128 == 0 and off + size <= tile else grain
                parts.append(tiles[b][:, off : off + step])
                at, size = at + step, size - step
            return parts[0] if len(parts) == 1 else jnp.concatenate(parts, axis=1)

        for p in range(n_item):
            def put(at, value):
                out_user[hop, p, at : at + value.shape[0], :] = value

            fold_in(put, lambda lane, size: lanes(p * piece_u + lane, size))
            send_now(RS_U, hop, p)
        in_user[hop, me_i] = out_user[hop, me_i]

    def item_terms(hop):
        end_gather(AG_U, hop)
        wires = [ag_user[hop, p] for p in range(n_item)]
        for at in range(0, n_item * piece_u, 128):
            p, lane = divmod(at, piece_u)
            if lane % 128 == 0 and lane < whole_lanes:
                block = unfold(wires[p], lane, 128)
            else:
                parts = []
                for g in range(at, at + 128, grain):
                    p, lane = divmod(g, piece_u)
                    parts.append(unfold(wires[p], lane, grain))
                block = jnp.concatenate(parts, axis=1)
            b, off = divmod(at, tile)
            user_panel[b, :, off : off + 128] = block
        for t in range(slots):
            to_item[t] = to_item[col_before[t]] + jnp.dot(
                user_panel[row_id[t]], adj[t], preferred_element_type=F32
            )
        for c in range(col_tiles):
            done = to_item[col_last[c]].astype(out_item.dtype)
            for lane in range(0, tile, 128):
                p, off = divmod(c * tile + lane, piece_i)
                out_item[hop, p, :, off : off + 128] = done[:, lane : lane + 128]
                if off + 128 == piece_i:
                    send_now(RS_I, hop, p)
        in_item[hop, me_u] = out_item[hop, me_u]

    def total(s, hop):
        end_settle(s, hop)
        dst = s[4]
        acc = dst[hop, 0].astype(F32)
        for p in range(1, s[2]):
            acc = acc + dst[hop, p].astype(F32)
        return acc

    user_terms(0)
    item_terms(0)
    once_i = total(RS_I, 0).astype(BF16)
    ag_item[1, me_u] = once_i
    start_gather(AG_I, 1)
    item_pack[1] = once_i
    once_u = total(RS_U, 0).astype(BF16)
    ag_user[1, me_i] = once_u
    start_gather(AG_U, 1)
    user_pack[1] = once_u
    user_terms(1)
    item_terms(1)

    def finish(s, packed):
        twice = total(s, 1)
        return ((packed[0].astype(F32) + packed[1].astype(F32) + twice) / 3.0).astype(BF16)

    item_grad[...] = finish(RS_I, item_pack)
    wire = finish(RS_U, user_pack)
    for lane in range(0, whole_lanes, 128):
        user_grad[:, lane : lane + 128] = unfold(wire, lane, 128)
    if whole_lanes < piece_u:
        user_grad[:, whole_lanes:piece_u] = unfold(wire, whole_lanes, grain)

    for hop in range(2):
        for g in (AG_U, AG_I):
            all_of(*g[:4], *g[3:], hop).wait_send()
        for s in (RS_U, RS_I):
            all_of(*s, hop).wait_send()


def shards(n_user, n_item, user_cot, item_cot, tile_weight, tile_rows, tile_cols, tile_count, user_degree, item_degree):
    slots, tile = tile_weight.shape[0], tile_weight.shape[2]
    width = user_cot.shape[1]
    shard_users, shard_items = user_degree.shape[0], item_degree.shape[0]
    row_tiles, col_tiles = shard_users // tile, shard_items // tile
    piece_u, piece_i = user_cot.shape[0], item_cot.shape[0]
    wire_u = (width * piece_u // 128, 128)
    wire_i = (width, piece_i)
    sizes = (n_user, n_item, slots, tile, width, row_tiles, col_tiles)
    sent = BF16
    vmem = pl.BlockSpec(memory_space=pltpu.VMEM)
    dma = pltpu.SemaphoreType.DMA
    user_grad, item_grad = pl.pallas_call(
        functools.partial(kernel, sizes),
        out_shape=(
            pltpu.VMEM((width, piece_u), BF16),
            pltpu.VMEM((width, piece_i), BF16),
        ),
        in_specs=[pl.BlockSpec(memory_space=pl.ANY)] * 8,
        out_specs=(vmem, vmem),
        scratch_shapes=[
            pltpu.VMEM((width, piece_u), BF16),
            pltpu.VMEM((width, piece_i), BF16),
            pltpu.VMEM((shard_users,), jnp.int32),
            pltpu.VMEM((shard_items,), jnp.int32),
            pltpu.SMEM(tile_rows.shape, jnp.int32),
            pltpu.SMEM(tile_cols.shape, jnp.int32),
            pltpu.SMEM(tile_count.shape, jnp.int32),
            pltpu.VMEM((slots, tile, tile), jnp.int32),
            pltpu.VMEM((slots, tile, tile), BF16),
            pltpu.VMEM((row_tiles, tile, 128), F32),
            pltpu.VMEM((col_tiles, 1, tile), F32),
            pltpu.VMEM((row_tiles, width, tile), BF16),
            pltpu.VMEM((col_tiles, width, tile), BF16),
            pltpu.VMEM((slots + 1, width, tile), F32),
            pltpu.VMEM((slots + 1, width, tile), F32),
            pltpu.VMEM((2, *wire_u), BF16),
            pltpu.VMEM((2, *wire_i), BF16),
            pltpu.VMEM((2, n_item, *wire_u), BF16),
            pltpu.VMEM((2, n_user, *wire_i), BF16),
            pltpu.VMEM((2, n_item, *wire_u), sent),
            pltpu.VMEM((2, n_user, *wire_i), sent),
            pltpu.VMEM((2, n_item, *wire_u), sent),
            pltpu.VMEM((2, n_user, *wire_i), sent),
            dma((slots,)), dma((7,)),
            *[dma((2,))] * 8,
        ],
        compiler_params=pltpu.CompilerParams(
            collective_id=0, has_side_effects=True, vmem_limit_bytes=60 * 1024 * 1024
        ),
    )(
        user_cot.T, item_cot.T, tile_weight, tile_rows, tile_cols, tile_count,
        user_degree, item_degree,
    )
    return user_grad.T, item_grad.T


def solution(mesh):
    return jax.shard_map(
        functools.partial(shards, mesh.shape["user"], mesh.shape["item"]),
        mesh=mesh,
        in_specs=(
            P(("user", "item"), None),
            P(("item", "user"), None),
            P("user", "item", None),
            P("user", "item"),
            P("user", "item"),
            P("user", "item"),
            P("user"),
            P("item"),
        ),
        out_specs=(P(("user", "item"), None), P(("item", "user"), None)),
        check_vma=False,
    )
```

```python
import functools
import math

import jax
import jax.numpy as jnp
from jax import lax
from jax.experimental import pallas as pl
from jax.experimental.pallas import tpu as pltpu
from jax.sharding import PartitionSpec as P

F32 = jnp.float32
BF16 = jnp.bfloat16
MESH = pl.DeviceIdType.MESH


def kernel(
    sizes, user_cot, item_cot, weight, rows_in, cols_in, count_in, user_deg, item_deg,
    user_grad, item_grad,
    cot_u, cot_i, deg_u, deg_i, rows, cols, count,
    raw, adj, row_scale, col_scale, user_panel, item_panel, to_user, to_item,
    user_pack, item_pack,
    ag_user, ag_item, out_user, out_item, in_user, in_item,
    load_sem, small_sem, ag_send_u, ag_recv_u, ag_send_i, ag_recv_i, rs_send_u, rs_recv_u, rs_send_i, rs_recv_i,
):
    n_user, n_item, slots, tile, width, row_tiles, col_tiles = sizes
    me_u, me_i = lax.axis_index("user"), lax.axis_index("item")
    piece_u, piece_i = cot_u.shape[1], cot_i.shape[1]

    small = [
        pltpu.make_async_copy(src, dst, small_sem.at[j])
        for j, (src, dst) in enumerate([
            (user_cot, cot_u), (item_cot, cot_i), (user_deg, deg_u), (item_deg, deg_i),
            (rows_in, rows), (cols_in, cols), (count_in, count),
        ])
    ]
    for copy in small[:2]:
        copy.start()
    barrier = pltpu.get_barrier_semaphore()

    def greet(axis, me, n):
        def step(k, carry):
            pl.semaphore_signal(
                barrier, inc=1, device_id={axis: lax.rem(me + k, n)}, device_id_type=MESH
            )
            return carry
        if n > 8:
            lax.fori_loop(1, n, step, 0)
        else:
            for k in range(1, n):
                step(k, 0)

    greet("item", me_i, n_item)
    greet("user", me_u, n_user)
    for copy in small[2:]:
        copy.start()
    for t in range(slots):
        pltpu.make_async_copy(weight.at[t], raw.at[t], load_sem.at[t]).start()


    grain = math.gcd(piece_u, 128)
    folds, whole_lanes = 128 // grain, piece_u // 128 * 128
    fold_rows, main_rows = width // folds, width * (piece_u // 128)

    def fold_in(put, take):
        for j in range(0, whole_lanes, 128):
            put(j // 128 * width, take(j, 128))
        if whole_lanes < piece_u:
            rest = take(whole_lanes, grain)
            put(main_rows, jnp.concatenate(
                [rest[f * fold_rows : (f + 1) * fold_rows, :] for f in range(folds)], axis=1))

    def unfold(wire, lane, size):
        if lane < whole_lanes:
            at = lane // 128 * width
            return wire[at : at + width, lane % 128 : lane % 128 + size]
        rest = wire[main_rows : main_rows + fold_rows, :]
        return jnp.concatenate(
            [rest[:, f * grain : (f + 1) * grain] for f in range(folds)], axis=0)

    for copy in small[:2]:
        copy.wait()
    own = cot_u[...]

    def put_own(at, value):
        user_pack[0, at : at + value.shape[0], :] = value

    fold_in(put_own, lambda lane, size: own[:, lane : lane + size])
    item_pack[0] = cot_i[...]
    ag_user[0, me_i] = user_pack[0]
    ag_item[0, me_u] = item_pack[0]

    pl.semaphore_wait(barrier, n_user + n_item - 2)

    def gather_copy(axis, me, n, buf, send, recv, hop, k):
        there = lax.rem(me + k, n)
        return pltpu.make_async_remote_copy(
            src_ref=buf.at[hop, me], dst_ref=buf.at[hop, me],
            send_sem=send.at[hop], recv_sem=recv.at[hop],
            device_id={axis: there}, device_id_type=MESH,
        )

    def settle_copy(axis, me, n, src, dst, send, recv, hop, k):
        there = lax.rem(me + k, n)
        return pltpu.make_async_remote_copy(
            src_ref=src.at[hop, there], dst_ref=dst.at[hop, me],
            send_sem=send.at[hop], recv_sem=recv.at[hop],
            device_id={axis: there}, device_id_type=MESH,
        )

    def all_of(axis, me, n, src, dst, send, recv, hop):
        return pltpu.make_async_remote_copy(
            src_ref=src.at[hop, pl.ds(0, n - 1)], dst_ref=dst.at[hop, pl.ds(0, n - 1)],
            send_sem=send.at[hop], recv_sem=recv.at[hop],
            device_id={axis: lax.rem(me + 1, n)}, device_id_type=MESH,
        )

    AG_U = ("item", me_i, n_item, ag_user, ag_send_u, ag_recv_u)
    AG_I = ("user", me_u, n_user, ag_item, ag_send_i, ag_recv_i)
    RS_U = ("item", me_i, n_item, out_user, in_user, rs_send_u, rs_recv_u)
    RS_I = ("user", me_u, n_user, out_item, in_item, rs_send_i, rs_recv_i)

    def each(n, fn):
        def step(k, carry):
            fn(k)
            return carry
        if n > 8:
            lax.fori_loop(1, n, step, 0)
        else:
            for k in [*range(2, n), 1] if n == n_user else range(1, n):
                fn(k)

    def start_gather(g, hop):
        each(g[2], lambda k: gather_copy(*g, hop, k).start())

    def end_gather(g, hop):
        all_of(*g[:4], *g[3:], hop).wait_recv()

    def start_settle(s, hop):
        each(s[2], lambda k: settle_copy(*s, hop, k).start())

    def send_now(s, hop, p):
        axis, me, n, src, dst, send, recv = s

        @pl.when(p != me)
        def _():
            pltpu.make_async_remote_copy(
                src_ref=src.at[hop, p], dst_ref=dst.at[hop, me],
                send_sem=send.at[hop], recv_sem=recv.at[hop],
                device_id={axis: jnp.int32(p)}, device_id_type=MESH,
            ).start()

    def end_settle(s, hop):
        all_of(*s, hop).wait_recv()

    start_gather(AG_I, 0)
    start_gather(AG_U, 0)

    for copy in small[2:]:
        copy.wait()
    for r in range(row_tiles):
        scale = lax.rsqrt(deg_u[r * tile : (r + 1) * tile].astype(F32)).reshape(1, tile)
        row_scale[r] = jnp.transpose(jnp.broadcast_to(scale, (128, tile)))
    for c in range(col_tiles):
        col_scale[c] = lax.rsqrt(deg_i[c * tile : (c + 1) * tile].astype(F32)).reshape(1, tile)
    row_id = [rows[0, t] for t in range(slots)]
    col_id = [cols[0, t] for t in range(slots)]

    def chain(ids, blocks):
        before = []
        for t in range(slots):
            prev = jnp.int32(slots)
            for s in range(t):
                prev = jnp.where(ids[s] == ids[t], jnp.int32(s), prev)
            before.append(prev)
        last = []
        for b in range(blocks):
            found = jnp.int32(slots)
            for t in range(slots):
                found = jnp.where(ids[t] == b, jnp.int32(t), found)
            last.append(found)
        return before, last

    row_before, row_last = chain(row_id, row_tiles)
    col_before, col_last = chain(col_id, col_tiles)
    to_user[slots] = jnp.zeros((width, tile), F32)
    to_item[slots] = jnp.zeros((width, tile), F32)
    live = count[0, 0]
    for t in range(slots):
        pltpu.make_async_copy(weight.at[t], raw.at[t], load_sem.at[t]).wait()
        on = jnp.where(t < live, jnp.float32(1), jnp.float32(0))
        rs = row_scale[row_id[t]]
        cs = col_scale[col_id[t]] * on
        w = raw[t].astype(F32)
        a = jnp.concatenate(
            [(w[:, j : j + 128] * rs) * cs[:, j : j + 128] for j in range(0, tile, 128)], axis=1
        ).astype(BF16)
        adj[t] = a

    def user_terms(hop):
        end_gather(AG_I, hop)
        for p in range(n_user):
            for lane in range(0, piece_i, 128):
                b, off = divmod(p * piece_i + lane, tile)
                item_panel[b, :, off : off + 128] = ag_item[hop, p, :, lane : lane + 128]
        for t in range(slots):
            to_user[t] = to_user[row_before[t]] + lax.dot_general(
                item_panel[col_id[t]], adj[t], (((1,), (1,)), ((), ())),
                preferred_element_type=F32,
            )
        tiles = [to_user[row_last[r]].astype(out_user.dtype) for r in range(row_tiles)]

        def lanes(at, size):
            parts = []
            while size:
                b, off = divmod(at, tile)
                step = size if off % 128 == 0 and off + size <= tile else grain
                parts.append(tiles[b][:, off : off + step])
                at, size = at + step, size - step
            return parts[0] if len(parts) == 1 else jnp.concatenate(parts, axis=1)

        for p in range(n_item):
            def put(at, value):
                out_user[hop, p, at : at + value.shape[0], :] = value

            fold_in(put, lambda lane, size: lanes(p * piece_u + lane, size))
            send_now(RS_U, hop, p)
        in_user[hop, me_i] = out_user[hop, me_i]

    def item_terms(hop):
        end_gather(AG_U, hop)
        wires = [ag_user[hop, p] for p in range(n_item)]
        for at in range(0, n_item * piece_u, 128):
            p, lane = divmod(at, piece_u)
            if lane % 128 == 0 and lane < whole_lanes:
                block = unfold(wires[p], lane, 128)
            else:
                parts = []
                for g in range(at, at + 128, grain):
                    p, lane = divmod(g, piece_u)
                    parts.append(unfold(wires[p], lane, grain))
                block = jnp.concatenate(parts, axis=1)
            b, off = divmod(at, tile)
            user_panel[b, :, off : off + 128] = block
        for t in range(slots):
            to_item[t] = to_item[col_before[t]] + jnp.dot(
                user_panel[row_id[t]], adj[t], preferred_element_type=F32
            )
        for c in range(col_tiles):
            done = to_item[col_last[c]].astype(out_item.dtype)
            for lane in range(0, tile, 128):
                p, off = divmod(c * tile + lane, piece_i)
                out_item[hop, p, :, off : off + 128] = done[:, lane : lane + 128]
                if off + 128 == piece_i:
                    send_now(RS_I, hop, p)
        in_item[hop, me_u] = out_item[hop, me_u]

    def total(s, hop):
        end_settle(s, hop)
        dst = s[4]
        acc = dst[hop, 0].astype(F32)
        for p in range(1, s[2]):
            acc = acc + dst[hop, p].astype(F32)
        return acc

    user_terms(0)
    item_terms(0)
    once_i = total(RS_I, 0).astype(BF16)
    ag_item[1, me_u] = once_i
    start_gather(AG_I, 1)
    item_pack[1] = once_i
    once_u = total(RS_U, 0).astype(BF16)
    ag_user[1, me_i] = once_u
    start_gather(AG_U, 1)
    user_pack[1] = once_u
    user_terms(1)
    item_terms(1)

    def finish(s, packed):
        twice = total(s, 1)
        return ((packed[0].astype(F32) + packed[1].astype(F32) + twice) / 3.0).astype(BF16)

    item_grad[...] = finish(RS_I, item_pack)
    wire = finish(RS_U, user_pack)
    for lane in range(0, whole_lanes, 128):
        user_grad[:, lane : lane + 128] = unfold(wire, lane, 128)
    if whole_lanes < piece_u:
        user_grad[:, whole_lanes:piece_u] = unfold(wire, whole_lanes, grain)

    for hop in range(2):
        for g in (AG_U, AG_I):
            all_of(*g[:4], *g[3:], hop).wait_send()
        for s in (RS_U, RS_I):
            all_of(*s, hop).wait_send()


def shards(n_user, n_item, user_cot, item_cot, tile_weight, tile_rows, tile_cols, tile_count, user_degree, item_degree):
    slots, tile = tile_weight.shape[0], tile_weight.shape[2]
    width = user_cot.shape[1]
    shard_users, shard_items = user_degree.shape[0], item_degree.shape[0]
    row_tiles, col_tiles = shard_users // tile, shard_items // tile
    piece_u, piece_i = user_cot.shape[0], item_cot.shape[0]
    wire_u = (width * piece_u // 128, 128)
    wire_i = (width, piece_i)
    sizes = (n_user, n_item, slots, tile, width, row_tiles, col_tiles)
    sent = BF16
    vmem = pl.BlockSpec(memory_space=pltpu.VMEM)
    dma = pltpu.SemaphoreType.DMA
    user_grad, item_grad = pl.pallas_call(
        functools.partial(kernel, sizes),
        out_shape=(
            pltpu.VMEM((width, piece_u), BF16),
            pltpu.VMEM((width, piece_i), BF16),
        ),
        in_specs=[pl.BlockSpec(memory_space=pl.ANY)] * 8,
        out_specs=(vmem, vmem),
        scratch_shapes=[
            pltpu.VMEM((width, piece_u), BF16),
            pltpu.VMEM((width, piece_i), BF16),
            pltpu.VMEM((shard_users,), jnp.int32),
            pltpu.VMEM((shard_items,), jnp.int32),
            pltpu.SMEM(tile_rows.shape, jnp.int32),
            pltpu.SMEM(tile_cols.shape, jnp.int32),
            pltpu.SMEM(tile_count.shape, jnp.int32),
            pltpu.VMEM((slots, tile, tile), jnp.int32),
            pltpu.VMEM((slots, tile, tile), BF16),
            pltpu.VMEM((row_tiles, tile, 128), F32),
            pltpu.VMEM((col_tiles, 1, tile), F32),
            pltpu.VMEM((row_tiles, width, tile), BF16),
            pltpu.VMEM((col_tiles, width, tile), BF16),
            pltpu.VMEM((slots + 1, width, tile), F32),
            pltpu.VMEM((slots + 1, width, tile), F32),
            pltpu.VMEM((2, *wire_u), BF16),
            pltpu.VMEM((2, *wire_i), BF16),
            pltpu.VMEM((2, n_item, *wire_u), BF16),
            pltpu.VMEM((2, n_user, *wire_i), BF16),
            pltpu.VMEM((2, n_item, *wire_u), sent),
            pltpu.VMEM((2, n_user, *wire_i), sent),
            pltpu.VMEM((2, n_item, *wire_u), sent),
            pltpu.VMEM((2, n_user, *wire_i), sent),
            dma((slots,)), dma((7,)),
            *[dma((2,))] * 8,
        ],
        compiler_params=pltpu.CompilerParams(
            collective_id=0, has_side_effects=True, vmem_limit_bytes=60 * 1024 * 1024
        ),
    )(
        user_cot.T, item_cot.T, tile_weight, tile_rows, tile_cols, tile_count,
        user_degree, item_degree,
    )
    return user_grad.T, item_grad.T


def solution(mesh):
    return jax.shard_map(
        functools.partial(shards, mesh.shape["user"], mesh.shape["item"]),
        mesh=mesh,
        in_specs=(
            P(("user", "item"), None),
            P(("item", "user"), None),
            P("user", "item", None),
            P("user", "item"),
            P("user", "item"),
            P("user", "item"),
            P("user"),
            P("item"),
        ),
        out_specs=(P(("user", "item"), None), P(("item", "user"), None)),
        check_vma=False,
    )
```
